256 devices in a mesh: out: 16 (over y, x), inp: 16 (over z, core).
Axes of the slice: x: 4, y: 4, z: 8, core: 2. Of those that a mesh axis runs over, the one named last changes fastest.
Arguments:
- grads: bfloat16 [2048, 28672], P('out', 'inp'), may hold values from -1.1953125 to 1.1953125
- acts: bfloat16 [2048, 8192], P('inp', 'out'), may hold values from -6 to 6
- basis_out: bfloat16 [28672, 14336], P('inp', 'out'), may hold values from -0.03125 to 0.03125
- basis_in: bfloat16 [8192, 8192], P('out', 'inp'), may hold values from -0.0625 to 0.0625
- old_correction: float32 [14336, 8192], P('out', 'inp'), may hold values from 0.1 to 2
- lengths: int32 [16], replicated, may hold values from 1 to 256, 2048 in all
Outputs:
- correction: float32 [14336, 8192], P('out', 'inp')
The draws below stay inside these ranges and needn't reach their ends.
Inputs may be any that keep to these rules, and one draw needn't show every extreme that they name: The lengths sum to 2048; the longest example has exactly 256 tokens.
All inputs are finite; a program needn't handle non-finite values.
Results may differ from the reference program's by a relative error of at most 0.0021.
Values may be sent and summed in bfloat16 or wider, within the bound.
No kernel may reach another device: no remote copies, remote signals or barrier semaphores. Data moves between devices by JAX's collectives and lax.ppermute only.
A program may use at most 128 MiB of HBM per device.

```python
import math
import jax
import jax.numpy as jnp
import numpy as np
from jax import lax

DOUT = 28672
DIN = 8192
KG = 14336
TOKENS = 2048
EX = 16
CAP = 256


def spiked(entries, key, source, target, blocks, factor):
    def block_of(axis_at):
        return (jnp.arange(entries.shape[axis_at]) // (entries.shape[axis_at] // blocks)).reshape((-1,) + (1,) * (entries.ndim - 1 - axis_at))

    near = jax.random.permutation(key, blocks)[block_of(target)]
    far = (block_of(target) + blocks // 2) % blocks
    return jnp.where((block_of(source) == near) | (block_of(source) == far), factor * entries, entries)


def levels(own_key, dims, split, least, largest):
    loudness = 1.0
    for dim, parts in split:
        heights = jax.random.uniform(jax.random.fold_in(jax.random.fold_in(own_key, 6), dim), (parts,), jnp.float32, least / len(split), largest / len(split))
        loudness = loudness * jnp.repeat(jnp.exp(heights), dims[dim] // parts).reshape((-1,) + (1,) * (len(dims) - 1 - dim))
    return loudness


def profile(amount, total, most, slope):
    loads = [(1 << 20) // math.isqrt(rank ** slope) + 1 for rank in range(2, amount + 1)]
    rest, holding = total - most - (amount - 1), [1] * (amount - 1)
    while rest > 0:
        candidates = [i for i in range(amount - 1) if holding[i] < most]
        pool, remaining = sum([loads[i] for i in candidates]), rest
        for i in candidates:
            extra = min(most - holding[i], max(1, remaining * loads[i] // pool), rest)
            holding[i] = holding[i] + extra
            rest = rest - extra
    return np.array([most] + holding)


def uneven_parts(rng, count, total, limit, lean):
    if count == 2:
        one = jax.random.randint(rng, (), max(1, total - limit), min(limit, total - 1) + 1)
        return jnp.stack([one, total - one])
    sizes = jnp.asarray(profile(count, total, limit, lean), jnp.int32)
    couples = (count - 1) // 2
    source_of, taker = sizes[1:1 + 2 * couples:2], sizes[2:2 + 2 * couples:2]
    margin = jnp.minimum(source_of - 1, limit - taker)
    shifted = jax.random.randint(jax.random.fold_in(rng, 1), (couples,), 0, 1 << 20) % (margin + 1)
    sizes = sizes.at[1:1 + 2 * couples:2].set(source_of - shifted).at[2:2 + 2 * couples:2].set(taker + shifted)
    return sizes[jax.random.permutation(jax.random.fold_in(rng, 2), count)]


def gaussian(rng, shape, scale, bound, shards=(), kind=jnp.bfloat16):
    level = levels(rng, shape, shards, -0.22, 0.18) if shards else 1.0
    result = jax.random.normal(rng, shape, jnp.float32) * scale * level
    return jnp.minimum(jnp.maximum(result, -bound), bound).astype(kind)


def bell_draw_with(key, shape, width, bound, cuts, heavy, kind=jnp.bfloat16):
    result = width * jax.random.normal(key, shape, jnp.float32)
    if cuts:
        result = result * levels(key, shape, cuts, -0.22, 0.18)
    return jnp.clip(spiked(result, jax.random.fold_in(key, 3), *heavy), -bound, bound).astype(kind)


def setup_inputs(seed: int = 0) -> dict:
    arg_keys = jax.random.split(jax.random.key(seed), 7)
    grads = bell_draw_with(arg_keys[0], (TOKENS, DOUT), 0.2, 1.1953125, ((0, 16), (1, 16)), (1, 0, 16, 2.0))
    acts = bell_draw_with(arg_keys[1], (TOKENS, DIN), 1.0, 6.0, ((0, 16), (1, 16)), (1, 0, 16, 2.0))
    basis_out = gaussian(arg_keys[2], (DOUT, KG), DOUT ** -0.5, 0.03125, ((0, 16), (1, 16)))
    basis_in = gaussian(arg_keys[3], (DIN, DIN), DIN ** -0.5, 0.0625, ((0, 16), (1, 16)))
    old_correction = jnp.clip(jnp.exp(math.log(2.0) - 2.9957323 * jax.random.uniform(arg_keys[4], (KG, DIN), jnp.float32) ** levels(arg_keys[4], (KG, DIN), ((0, 16), (1, 16)), -0.2, 0.2)), 0.1, 2.0)
    lengths = uneven_parts(arg_keys[5], EX, TOKENS, CAP, 2).astype(jnp.int32)
    return dict(grads=grads, acts=acts, basis_out=basis_out, basis_in=basis_in, old_correction=old_correction, lengths=lengths)


def reference(grads, acts, basis_out, basis_in, old_correction, lengths):
    grad_rot = jnp.dot(grads, basis_out, preferred_element_type=jnp.float32).astype(jnp.bfloat16)
    act_rot = jnp.dot(acts, basis_in, preferred_element_type=jnp.float32).astype(jnp.bfloat16)
    offsets = (jnp.cumsum(lengths) - lengths).astype(jnp.int32)
    row_count = grads.shape[0]

    def add_example(example, running):
        offset = offsets[example]
        length = lengths[example]
        first_row = jnp.minimum(offset, row_count - CAP).astype(jnp.int32)
        places = first_row + jnp.arange(CAP, dtype=jnp.int32)
        inside = (places >= offset) & (places < offset + length)
        grad_block = lax.dynamic_slice_in_dim(grad_rot, first_row, CAP, 0)
        act_block = lax.dynamic_slice_in_dim(act_rot, first_row, CAP, 0)
        act_block = jnp.where(inside[:, None], act_block, jnp.zeros((), act_block.dtype))
        projected = lax.dot_general(grad_block, act_block, (((0,), (0,)), ((), ())), preferred_element_type=jnp.float32)
        return running + projected * projected

    running = lax.fori_loop(0, EX, add_example, jnp.zeros(old_correction.shape, jnp.float32))
    return 0.8 * old_correction + 0.2 * running / EX
```

```python
import jax
import jax.numpy as jnp
from jax import lax
from jax.experimental import pallas as pl
from jax.experimental.pallas import tpu as pltpu
from jax.sharding import PartitionSpec as P

CAP = 256
X = Y = 4
Z = 8
PIECE = 64
ALIGN = 16
STEPS = (0, -1, 1, 2)
WIRE = jnp.float16
GRAD_SCALE = 32.0
ACT_SCALE = 16.0


def move_out(array, dx, dy):
    pairs = [
        (y * X + x, (y + dy) % Y * X + (x + dx) % X) for y in range(Y) for x in range(X)
    ]
    return lax.ppermute(array, "out", pairs)


def move_x(array, step):
    return move_out(array, step, 0)


def move_y(array, step):
    return move_out(array, 0, step)


def move_z(array, step):
    pairs = [(z * 2 + c, (z + step) % Z * 2 + c) for z in range(Z) for c in range(2)]
    return lax.ppermute(array, "inp", pairs)


def swap_cores(array):
    pairs = [(z * 2 + c, z * 2 + 1 - c) for z in range(Z) for c in range(2)]
    return lax.ppermute(array, "inp", pairs)


def gather4(move, block):
    half = block.shape[0] // 2
    right, left = move(block, 1), move(block, -1)
    right2, left2 = move(right[:half], 1), move(left[half:], -1)
    return [block, right, left, right2, left2]


def gather8(move, block):
    half = block.shape[0] // 2
    right, left = block, block
    blocks = [block]
    for _ in range(3):
        right, left = move(right, 1), move(left, -1)
        blocks += [right, left]
    return blocks + [move(right[:half], 1), move(left[half:], -1)]


def narrow(array, scale):
    return (array * scale).astype(WIRE)


def wide(array, scale):
    return array.astype(jnp.float32) * (1.0 / scale)


def scatter_sum(move, part, count, scale):
    far = count // 2
    term = part(far)
    half = term.shape[0] // 2
    right, left = move(narrow(term[:half], scale), 1), move(narrow(term[half:], scale), -1)
    zero = jnp.zeros_like(right)
    right, left = jnp.concatenate([right, zero]), jnp.concatenate([zero, left])
    for k in range(far - 1, 0, -1):
        right = move(narrow(wide(right, scale) + part(k), scale), 1)
        left = move(narrow(wide(left, scale) + part(-k), scale), -1)
    return wide(right, scale) + wide(left, scale) + part(0)


def final_kernel(dest_g, dest_a, offsets, lengths, g0, g1, a0, a1, old, out, gs, acs):
    per_set = g0.shape[0] // PIECE
    for piece in range(2 * per_set):
        rows = pl.ds(piece % per_set * PIECE, PIECE)
        place = pl.ds(pl.multiple_of(dest_g[piece] * PIECE, PIECE), PIECE)
        gs[place, :] = (g0, g1)[piece // per_set][rows, :]
        place = pl.ds(pl.multiple_of(dest_a[piece] * PIECE, PIECE), PIECE)
        acs[place, :] = (a0, a1)[piece // per_set][rows, :]
    out[...] = jnp.zeros_like(out)
    row_count = gs.shape[0]
    tile = 128

    def add_example(first, offset, length, count):
        window = pl.ds(first, count)
        act = acs[window, :]
        places = first + lax.broadcasted_iota(jnp.int32, act.shape, 0)
        inside = (places >= offset) & (places < offset + length)
        act = jnp.where(inside, act.astype(jnp.float32), 0.0).astype(jnp.bfloat16)
        for start in range(0, out.shape[0], tile):
            projected = lax.dot_general(
                gs[window, start : start + tile],
                act,
                (((0,), (0,)), ((), ())),
                preferred_element_type=jnp.float32,
            )
            out[start : start + tile, :] += projected * projected

    @pl.loop(0, offsets.shape[0])
    def _(example):
        offset, length = offsets[example], lengths[example]
        first = jnp.minimum(offset // ALIGN * ALIGN, row_count - CAP)
        first = pl.multiple_of(first, ALIGN)
        fits = offset + length <= first + CAP

        @pl.when(fits)
        def _():
            add_example(first, offset, length, CAP)

        @pl.when(jnp.logical_not(fits))
        def _():
            add_example(first, offset, length, CAP + ALIGN)

    out[...] = 0.8 * old[...] + 0.2 * out[...] / offsets.shape[0]


def correct(dest_g, dest_a, offsets, lengths, g0, g1, a0, a1, old):
    smem = pl.BlockSpec(memory_space=pltpu.SMEM)
    vmem = pl.BlockSpec(memory_space=pltpu.VMEM)
    rows = 2 * g0.shape[0]
    return pl.pallas_call(
        final_kernel,
        out_shape=jax.ShapeDtypeStruct(old.shape, jnp.float32),
        in_specs=[smem] * 4 + [vmem] * 5,
        out_specs=vmem,
        scratch_shapes=[
            pltpu.VMEM((rows, g0.shape[1]), jnp.bfloat16),
            pltpu.VMEM((rows, a0.shape[1]), jnp.bfloat16),
        ],
        compiler_params=pltpu.CompilerParams(vmem_limit_bytes=48 * 2**20),
    )(dest_g, dest_a, offsets, lengths, g0, g1, a0, a1, old)


def slab(array, index, count):
    rows = array.shape[0] // count
    return lax.dynamic_slice_in_dim(array, index % count * rows, rows)


def body(grads, acts, basis_out, basis_in, old_correction, lengths):
    out_at, inp_at = lax.axis_index("out"), lax.axis_index("inp")
    y_at, x_at, z_at, core = out_at // X, out_at % X, inp_at // 2, inp_at % 2
    steps = jnp.array(STEPS, jnp.int32)
    xs, ys = (x_at + steps) % X, (y_at + steps) % Y

    all_acts = lax.all_gather(acts, "inp", axis=0, tiled=True)

    half = grads.shape[0] // 2
    first = jnp.concatenate(gather4(move_x, grads[:half]))
    second = jnp.concatenate(gather4(move_y, grads[half:]))
    sets = gather4(move_y, first), gather4(move_x, second)

    def rotate(blocks):
        return jnp.concatenate(
            [jnp.dot(b, basis_out, preferred_element_type=jnp.float32) for b in blocks]
        )

    rot0, rot1 = rotate(sets[0]), rotate(sets[1])
    keep = jnp.where(core == 0, rot0, rot1)
    give = jnp.where(core == 0, rot1, rot0)
    keep = keep + wide(swap_cores(narrow(give, GRAD_SCALE)), GRAD_SCALE)
    mine = scatter_sum(move_z, lambda k: slab(keep, z_at + k, Z), Z, GRAD_SCALE)
    own = jnp.concatenate(gather8(move_z, mine.astype(jnp.bfloat16)))
    other = swap_cores(own)

    act_part = jnp.dot(all_acts, basis_in, preferred_element_type=jnp.float32)
    part0, part1 = jnp.split(act_part, 2)
    sum0 = scatter_sum(move_x, lambda k: slab(part0, x_at + k, X), X, ACT_SCALE)
    sum1 = scatter_sum(move_y, lambda k: slab(part1, y_at + k, Y), Y, ACT_SCALE)
    sum0 = scatter_sum(move_y, lambda k: slab(sum0, y_at + k, Y), Y, ACT_SCALE)
    sum1 = scatter_sum(move_x, lambda k: slab(sum1, x_at + k, X), X, ACT_SCALE)
    act0 = jnp.concatenate(gather4(move_y, sum0.astype(jnp.bfloat16)))
    act1 = jnp.concatenate(gather4(move_x, sum1.astype(jnp.bfloat16)))
    act0 = jnp.concatenate(gather4(move_x, act0))
    act1 = jnp.concatenate(gather4(move_y, act1))

    set0 = (2 * (ys[:, None] * X + xs[None, :])).reshape(-1)
    set1 = (2 * (ys[None, :] * X + xs[:, None]) + 1).reshape(-1)
    zs = jnp.stack([z_at, z_at - 1, z_at + 1, z_at - 2, z_at + 2, z_at - 3, z_at + 3, z_at + 4]) % Z
    chunk = (2 * zs[:, None] + jnp.arange(2)[None, :]).reshape(-1)
    dest_own = jnp.where(core == 0, set0, set1)[chunk]
    dest_other = jnp.where(core == 0, set1, set0)[chunk]
    dest_g = jnp.concatenate([dest_own, dest_other]).astype(jnp.int32)
    place0 = (4 * xs[:, None] + ys[None, :]).reshape(-1)
    place1 = (16 + 4 * ys[:, None] + xs[None, :]).reshape(-1)
    dest_a = jnp.concatenate([place0, place1]).astype(jnp.int32)

    offsets = (jnp.cumsum(lengths) - lengths).astype(jnp.int32)
    return correct(dest_g, dest_a, offsets, lengths, own, other, act0, act1, old_correction)


def solution(mesh):
    in_specs = (
        P("out", "inp"),
        P("inp", "out"),
        P("inp", "out"),
        P("out", "inp"),
        P("out", "inp"),
        P(),
    )
    out_specs = P("out", "inp")
    return jax.shard_map(body, mesh=mesh, in_specs=in_specs, out_specs=out_specs, check_vma=False)
```

```python
import functools

import jax
import jax.numpy as jnp
from jax import lax
from jax.experimental import pallas as pl
from jax.experimental.pallas import tpu as pltpu
from jax.sharding import PartitionSpec as P

CAP = 256
X = Y = 4
Z = 8
PIECE = 128
ALIGN = 16
STEPS = (0, -1, 1, 2)
WIRE = jnp.float16
GIVE = jnp.bfloat16
GRAD_SCALE = 32.0
ACT_SCALE = 16.0


def place():
    out, inp = lax.axis_index("out"), lax.axis_index("inp")
    return lax.rem(out, X), out // X, inp // 2, lax.rem(inp, 2)


def move_plane(array, step, axes):
    mesh_out, mesh_inp = X * Y, 2 * Z
    pairs = []
    for y in range(Y):
        for x in range(X):
            near = {"x": y * X + (x + step) % X, "y": (y + step) % Y * X + x}
            for inp in range(mesh_inp):
                pairs.append(((y * X + x) * mesh_inp + inp, near[axes[inp % 2]] * mesh_inp + inp))
    return lax.ppermute(array, ("out", "inp"), pairs)


def move_first(array, step):
    return move_plane(array, step, "xy")


def move_second(array, step):
    return move_plane(array, step, "yx")


def move_z(array, step):
    pairs = [(z * 2 + c, (z + step) % Z * 2 + c) for z in range(Z) for c in range(2)]
    return lax.ppermute(array, "inp", pairs)


def move_apart(array):
    pairs = [(z * 2 + c, (z + 1 - 2 * c) % Z * 2 + c) for z in range(Z) for c in range(2)]
    return lax.ppermute(array, "inp", pairs)


def swap_cores(array):
    pairs = [(z * 2 + c, z * 2 + 1 - c) for z in range(Z) for c in range(2)]
    return lax.ppermute(array, "inp", pairs)


def gather4(move, first, second):
    right, left = move(first, 1), move(second, -1)
    right_rest, left_rest = move(second, 1), move(first, -1)
    right2, left2 = move(right, 1), move(left, -1)
    return [first, second, right, right_rest, left_rest, left, right2, left2]


def gather8(move, block, waits):
    half = block.shape[0] // 2
    right, left = block, block
    blocks = [block]
    for step in range(3):
        right, left = move(right, 1), move(left, -1)
        blocks += [right, left]
        mark = waits(step, blocks)
        if mark is not None:
            right, left = after((right, left), mark)
    return blocks, [move(right[:half], 1), move(left[half:], -1)]


def pack_kernel(*refs):
    *parts, out, sems = refs
    copies, row = [], 0
    for i, part in enumerate(parts):
        rows = pl.ds(row, part.shape[0])
        copies.append(pltpu.make_async_copy(part, out.at[rows, :], sems.at[i]))
        row += part.shape[0]
    for copy in copies:
        copy.start()
    for copy in copies:
        copy.wait()


def pack(blocks):
    rows = sum(b.shape[0] for b in blocks)
    like = blocks[0]
    anywhere = pl.BlockSpec(memory_space=pl.ANY)
    hbm = pl.BlockSpec(memory_space=pltpu.HBM)
    return pl.pallas_call(
        pack_kernel,
        out_shape=jax.ShapeDtypeStruct((rows, like.shape[1]), like.dtype),
        in_specs=[anywhere] * len(blocks),
        out_specs=hbm,
        scratch_shapes=[pltpu.SemaphoreType.DMA((len(blocks),))],
        compiler_params=pltpu.CompilerParams(vmem_limit_bytes=2**20),
        cost_estimate=pl.CostEstimate(
            flops=0, bytes_accessed=4 * rows * like.shape[1], transcendentals=0
        ),
    )(*blocks)


def rotate_kernel(*refs):
    *blocks, basis, out, total, sems = refs
    copies, row = [], 0
    for i, block in enumerate(blocks):
        rows = pl.ds(row, block.shape[0])
        total[rows, :] = jnp.dot(block[...], basis[...], preferred_element_type=jnp.float32)
        copies.append(pltpu.make_async_copy(total.at[rows, :], out.at[rows, :], sems.at[i]))
        copies[-1].start()
        row += block.shape[0]
    for copy in copies:
        copy.wait()


def rotate(blocks, basis):
    rows, columns = sum(b.shape[0] for b in blocks), basis.shape[1]
    vmem = pl.BlockSpec(memory_space=pltpu.VMEM)
    size = 2 * (rows + columns) * basis.shape[0] + 4 * rows * columns
    return pl.pallas_call(
        rotate_kernel,
        out_shape=jax.ShapeDtypeStruct((rows, columns), jnp.float32),
        in_specs=[vmem] * (len(blocks) + 1),
        out_specs=pl.BlockSpec(memory_space=pltpu.HBM),
        scratch_shapes=[
            pltpu.VMEM((rows, columns), jnp.float32),
            pltpu.SemaphoreType.DMA((len(blocks),)),
        ],
        compiler_params=pltpu.CompilerParams(vmem_limit_bytes=size + 4 * 2**20),
        cost_estimate=pl.CostEstimate(
            flops=2 * rows * basis.shape[0] * columns, bytes_accessed=size, transcendentals=0
        ),
    )(*blocks, basis)


def narrow(array, scale):
    return (array * scale).astype(WIRE)


def wide(array, scale):
    return array.astype(jnp.float32) * (1.0 / scale)


def after(pair, mark):
    marks = mark if isinstance(mark, list) else [mark]
    return lax.optimization_barrier((*pair, *marks))[: len(pair)]


def scatter_sum(move, part, count, scale, waits):
    far = count // 2
    term = part(far)
    half = term.shape[0] // 2
    right, left = narrow(term[:half], scale), narrow(term[half:], scale)
    for k in range(far - 1, -1, -1):
        mark = waits(far - 1 - k, right)
        right, left = move(right, 1), move(left, -1)
        if mark is not None:
            right, left = after((right, left), mark)
        if k == far - 1:
            zero = jnp.zeros_like(right)
            right, left = jnp.concatenate([right, zero]), jnp.concatenate([zero, left])
        if k == 0:
            break
        right = narrow(wide(right, scale) + part(k), scale)
        left = narrow(wide(left, scale) + part(-k), scale)
    return wide(right, scale) + wide(left, scale) + part(0)


def step_of(index):
    return jnp.where(index == 3, 2, jnp.where(index == 2, 1, -index))


def final_kernel(lengths, *refs):
    own, (near, right, left), acts, (old, out, gs, acs, sems) = refs[:9], refs[9:12], refs[12:16], refs[16:]
    x, y, z, core = place()
    copies = []

    def fetch(source, row, count, whole, start):
        start = pl.multiple_of(start, PIECE // 2)
        copies.append(
            pltpu.make_async_copy(
                source.at[pl.ds(row, count), :], whole.at[pl.ds(start, count), :], sems.at[len(copies)]
            )
        )
        copies[-1].start()

    def fetch_grads(block, row, count, chunk, holder, into):
        grid_row, column = chunk // 4 + 2 * holder, lax.rem(chunk, 4)
        piece = lax.rem(y + step_of(grid_row) + Y, Y) * X + lax.rem(x + step_of(column) + X, X)
        fetch(block, row, count, gs, piece * PIECE + into)

    for i, step in enumerate((0, -1, 1, -2, 2, -3, 3)):
        chunk = lax.rem(z + step + Z, Z)
        fetch_grads(own[i], 0, PIECE, chunk, core, 0)
        fetch_grads(near, i * PIECE, PIECE, chunk, 1 - core, 0)
    far = lax.rem(z + Z // 2, Z)
    for holder, halves in ((core, own[7:]), (1 - core, (right, left))):
        for i, half in enumerate(halves):
            fetch_grads(half, 0, PIECE // 2, far, holder, i * (PIECE // 2))
    first_at, second_at = jnp.where(core == 0, x, y), jnp.where(core == 0, y, x)
    way = 1 - 2 * core
    for i, block in enumerate(acts):
        for k in range(4):
            piece = lax.rem(first_at + STEPS[i] + 4, 4) * 4 + lax.rem(second_at + STEPS[k] + 4, 4)
            theirs = piece - 9
            at = jnp.where(piece < 9, z - way * (piece // 2), z + way * (theirs // 2 + 1))
            odd = jnp.where(piece < 9, lax.rem(piece, 2), 1 - lax.rem(theirs + 16, 2))
            holder = jnp.where(odd == 0, core, 1 - core)
            fetch(block, k * PIECE, PIECE, acs, (lax.rem(at + Z, Z) * 2 + holder) * PIECE)
    for copy in copies:
        copy.wait()
    out[...] = jnp.zeros_like(out)
    row_count = gs.shape[0]
    tile = 128

    def add_example(first, offset, length, count):
        window = pl.ds(first, count)
        act = acs[window, :]
        places = first + lax.broadcasted_iota(jnp.int32, act.shape, 0)
        inside = (places >= offset) & (places < offset + length)
        act = jnp.where(inside, act.astype(jnp.float32), 0.0).astype(jnp.bfloat16)
        for start in range(0, out.shape[0], tile):
            projected = lax.dot_general(
                gs[window, start : start + tile],
                act,
                (((0,), (0,)), ((), ())),
                preferred_element_type=jnp.float32,
            )
            out[start : start + tile, :] += projected * projected

    def step(example, offset):
        length = lengths[example]
        first = jnp.minimum(offset // ALIGN * ALIGN, row_count - CAP)
        first = pl.multiple_of(first, ALIGN)
        fits = offset + length <= first + CAP

        @pl.when(fits)
        def _():
            add_example(first, offset, length, CAP)

        @pl.when(jnp.logical_not(fits))
        def _():
            add_example(first, offset, length, CAP + ALIGN)

        return offset + length

    lax.fori_loop(0, lengths.shape[0], step, jnp.int32(0))
    out[...] = 0.8 * old[...] + 0.2 * out[...] / lengths.shape[0]


def correct(lengths, grads, acts, old):
    rows = sum(b.shape[0] for b in acts)
    smem = pl.BlockSpec(memory_space=pltpu.SMEM)
    vmem = pl.BlockSpec(memory_space=pltpu.VMEM)
    hbm = pl.BlockSpec(memory_space=pltpu.HBM)
    return pl.pallas_call(
        final_kernel,
        out_shape=jax.ShapeDtypeStruct(old.shape, jnp.float32),
        in_specs=[smem] + [hbm] * (len(grads) + len(acts)) + [vmem],
        out_specs=vmem,
        scratch_shapes=[
            pltpu.VMEM((rows, grads[0].shape[1]), jnp.bfloat16),
            pltpu.VMEM((rows, acts[0].shape[1]), jnp.bfloat16),
            pltpu.SemaphoreType.DMA((2 * 9 + X * Y,)),
        ],
        compiler_params=pltpu.CompilerParams(vmem_limit_bytes=60 * 2**20),
    )(lengths, *grads, *acts, old)


def divide_kernel(y0, y12, right, left, basis, give, keep, y3, give_at, keep_at, sems):
    half = right.shape[0]
    y3[:half, :] = jnp.dot(right[...], basis[...], preferred_element_type=jnp.float32)
    y3[half:, :] = jnp.dot(left[...], basis[...], preferred_element_type=jnp.float32)
    rows = y0.shape[0] // 4
    core = place()[3]

    def piece(row, column, mine):
        i, k = (row, column) if mine == 0 else (column, row)
        block, start = ((y0, 0), (y12, 0), (y12, 4), (y3, 0))[i]
        return block[(start + k) * rows : (start + k + 1) * rows, :]

    for mine in range(2):

        @pl.when(core == mine)
        def _():
            for k in range(8):
                here = slice(k * rows, (k + 1) * rows)
                give_at[here, :] = piece(k // 4 + 2 - 2 * mine, k % 4, mine).astype(give.dtype)

    given = pltpu.make_async_copy(give_at, give, sems.at[0])
    given.start()
    for mine in range(2):

        @pl.when(core == mine)
        def _():
            for k in range(8):
                here = slice(k * rows, (k + 1) * rows)
                keep_at[here, :] = piece(k // 4 + 2 * mine, k % 4, mine)

    kept = pltpu.make_async_copy(keep_at, keep, sems.at[1])
    kept.start()
    given.wait()
    kept.wait()


def divide(done, right, left, basis):
    rows, columns = 2 * done[0].shape[0], basis.shape[1]
    vmem = pl.BlockSpec(memory_space=pltpu.VMEM)
    hbm = pl.BlockSpec(memory_space=pltpu.HBM)
    return pl.pallas_call(
        divide_kernel,
        out_shape=[
            jax.ShapeDtypeStruct((rows, columns), GIVE),
            jax.ShapeDtypeStruct((rows, columns), jnp.float32),
        ],
        in_specs=[vmem] * 5,
        out_specs=[hbm, hbm],
        scratch_shapes=[
            pltpu.VMEM(done[0].shape, jnp.float32),
            pltpu.VMEM((rows, columns), GIVE),
            pltpu.VMEM((rows, columns), jnp.float32),
            pltpu.SemaphoreType.DMA((2,)),
        ],
        compiler_params=pltpu.CompilerParams(vmem_limit_bytes=24 * 2**20),
        cost_estimate=pl.CostEstimate(
            flops=rows * basis.shape[0] * columns,
            bytes_accessed=16 * rows * columns,
            transcendentals=0,
        ),
    )(*done, right, left, basis)


def slab(array, index, count):
    rows = array.shape[0] // count
    return lax.dynamic_slice_in_dim(array, index % count * rows, rows)


def body(grads, acts, basis_out, basis_in, old_correction, lengths):
    x_at, y_at, z_at, core = place()
    first_at = jnp.where(core == 0, x_at, y_at)
    second_at = jnp.where(core == 0, y_at, x_at)

    half = grads.shape[0] // 2
    inner = gather4(move_first, grads[:half], grads[half:])
    outer = pack(inner[:4]), pack(inner[4:])
    blocks = gather4(move_second, *outer)
    done = [rotate(outer, basis_out), rotate(blocks[2:6], basis_out)]

    both = pack([acts, swap_cores(acts)])
    steps = [move_apart(both)]
    steps.append(move_apart(steps[-1]))
    steps += after([steps.pop()], done[0])
    steps.append(move_apart(steps[-1]))
    steps.append(move_apart(steps[-1][: acts.shape[0]]))
    passed = pack(steps)
    all_acts = [both, passed, swap_cores(passed)]
    act_part = rotate(all_acts, basis_in)
    act_terms = [narrow(slab(act_part, first_at + k, 4), ACT_SCALE) for k in (1, -1, 2)]
    last = after(blocks[6:], act_terms[0])
    give, keep = divide(done, *last, basis_out)
    got = swap_cores(give)
    act = {"moved": [move_first(t, k) for t, k in zip(act_terms, (1, -1, 2))]}

    def act_sums(step, sent):
        if step == 1:
            moved = after(act["moved"], sent)
            sums = sum((wide(t, ACT_SCALE) for t in moved), slab(act_part, first_at, 4))
            terms = [narrow(slab(sums, second_at + k, 4), ACT_SCALE) for k in (1, -1, 2)]
            act["moved"] = [move_second(t, k) for t, k in zip(terms, (1, -1, 2))]
            act["sums"] = sums
            return terms[0]
        if step == 2:
            moved = after(act["moved"], sent)
            sums = sum((wide(t, ACT_SCALE) for t in moved), slab(act["sums"], second_at, 4))
            sums = sums.astype(jnp.bfloat16)
            act["moved"] = [move_second(sums, k) for k in (1, -1, 2)]
            act["sums"] = sums
            return sums
        if step == 3:
            sums = pack([act["sums"], *after(act["moved"], sent)])
            act["blocks"] = [sums, *[move_first(sums, k) for k in (1, -1, 2)]]
            return sums
        return None

    mine = scatter_sum(
        move_z,
        lambda k: slab(keep, z_at + k, Z) + slab(got, z_at + k, Z).astype(jnp.float32),
        Z,
        GRAD_SCALE,
        act_sums,
    )
    act_blocks = act["blocks"]

    near, far = gather8(
        move_z,
        mine.astype(jnp.bfloat16),
        lambda step, blocks: act_blocks[1:] if step == 1 else None,
    )
    grad_blocks = [*near, *far, swap_cores(pack(near)), *map(swap_cores, far)]
    return correct(lengths, grad_blocks, act_blocks, old_correction)


def solution(mesh):
    in_specs = (
        P("out", "inp"),
        P("inp", "out"),
        P("inp", "out"),
        P("out", "inp"),
        P("out", "inp"),
        P(),
    )
    out_specs = P("out", "inp")
    return jax.shard_map(body, mesh=mesh, in_specs=in_specs, out_specs=out_specs, check_vma=False)
```

```python
import functools

import jax
import jax.numpy as jnp
from jax import lax
from jax.experimental import pallas as pl
from jax.experimental.pallas import tpu as pltpu
from jax.sharding import PartitionSpec as P

CAP = 256
X = Y = 4
Z = 8
PIECE = 128
ALIGN = 16
STEPS = (0, -1, 1, 2)
WIRE = jnp.float16
GIVE = jnp.bfloat16
GRAD_SCALE = 32.0
ACT_SCALE = 16.0


def place():
    out, inp = lax.axis_index("out"), lax.axis_index("inp")
    return lax.rem(out, X), out // X, inp // 2, lax.rem(inp, 2)


def move_plane(array, step, axes):
    mesh_out, mesh_inp = X * Y, 2 * Z
    pairs = []
    for y in range(Y):
        for x in range(X):
            near = {"x": y * X + (x + step) % X, "y": (y + step) % Y * X + x}
            for inp in range(mesh_inp):
                pairs.append(((y * X + x) * mesh_inp + inp, near[axes[inp % 2]] * mesh_inp + inp))
    return lax.ppermute(array, ("out", "inp"), pairs)


def move_first(array, step):
    return move_plane(array, step, "xy")


def move_second(array, step):
    return move_plane(array, step, "yx")


def move_z(array, step):
    pairs = [(z * 2 + c, (z + step) % Z * 2 + c) for z in range(Z) for c in range(2)]
    return lax.ppermute(array, "inp", pairs)


def move_apart(array):
    pairs = [(z * 2 + c, (z + 1 - 2 * c) % Z * 2 + c) for z in range(Z) for c in range(2)]
    return lax.ppermute(array, "inp", pairs)


def swap_cores(array):
    pairs = [(z * 2 + c, z * 2 + 1 - c) for z in range(Z) for c in range(2)]
    return lax.ppermute(array, "inp", pairs)


def gather4(move, first, second):
    right, left = move(first, 1), move(second, -1)
    right_rest, left_rest = move(second, 1), move(first, -1)
    right2, left2 = move(right, 1), move(left, -1)
    return [first, second, right, right_rest, left_rest, left, right2, left2]


def gather8(move, block, waits):
    half = block.shape[0] // 2
    right, left = block, block
    blocks = [block]
    for step in range(3):
        right, left = move(right, 1), move(left, -1)
        blocks += [right, left]
        mark = waits(step, blocks)
        if mark is not None:
            right, left = after((right, left), mark)
    return blocks, [move(right[:half], 1), move(left[half:], -1)]


def pack_kernel(*refs):
    *parts, out, sems = refs
    copies, row = [], 0
    for i, part in enumerate(parts):
        rows = pl.ds(row, part.shape[0])
        copies.append(pltpu.make_async_copy(part, out.at[rows, :], sems.at[i]))
        row += part.shape[0]
    for copy in copies:
        copy.start()
    for copy in copies:
        copy.wait()


def pack(blocks):
    rows = sum(b.shape[0] for b in blocks)
    like = blocks[0]
    anywhere = pl.BlockSpec(memory_space=pl.ANY)
    hbm = pl.BlockSpec(memory_space=pltpu.HBM)
    return pl.pallas_call(
        pack_kernel,
        out_shape=jax.ShapeDtypeStruct((rows, like.shape[1]), like.dtype),
        in_specs=[anywhere] * len(blocks),
        out_specs=hbm,
        scratch_shapes=[pltpu.SemaphoreType.DMA((len(blocks),))],
        compiler_params=pltpu.CompilerParams(vmem_limit_bytes=2**20),
        cost_estimate=pl.CostEstimate(
            flops=0, bytes_accessed=4 * rows * like.shape[1], transcendentals=0
        ),
    )(*blocks)


def rotate_kernel(*refs):
    *blocks, basis, out, total, sems = refs
    copies, row = [], 0
    for i, block in enumerate(blocks):
        rows = pl.ds(row, block.shape[0])
        total[rows, :] = jnp.dot(block[...], basis[...], preferred_element_type=jnp.float32)
        copies.append(pltpu.make_async_copy(total.at[rows, :], out.at[rows, :], sems.at[i]))
        copies[-1].start()
        row += block.shape[0]
    for copy in copies:
        copy.wait()


def rotate(blocks, basis):
    rows, columns = sum(b.shape[0] for b in blocks), basis.shape[1]
    vmem = pl.BlockSpec(memory_space=pltpu.VMEM)
    size = 2 * (rows + columns) * basis.shape[0] + 4 * rows * columns
    return pl.pallas_call(
        rotate_kernel,
        out_shape=jax.ShapeDtypeStruct((rows, columns), jnp.float32),
        in_specs=[vmem] * (len(blocks) + 1),
        out_specs=pl.BlockSpec(memory_space=pltpu.HBM),
        scratch_shapes=[
            pltpu.VMEM((rows, columns), jnp.float32),
            pltpu.SemaphoreType.DMA((len(blocks),)),
        ],
        compiler_params=pltpu.CompilerParams(vmem_limit_bytes=size + 4 * 2**20),
        cost_estimate=pl.CostEstimate(
            flops=2 * rows * basis.shape[0] * columns, bytes_accessed=size, transcendentals=0
        ),
    )(*blocks, basis)


def narrow(array, scale):
    return (array * scale).astype(WIRE)


def wide(array, scale):
    return array.astype(jnp.float32) * (1.0 / scale)


def after(pair, mark):
    marks = mark if isinstance(mark, list) else [mark]
    return lax.optimization_barrier((*pair, *marks))[: len(pair)]


def scatter_sum(move, part, count, scale, waits):
    far = count // 2
    term = part(far)
    half = term.shape[0] // 2
    right, left = narrow(term[:half], scale), narrow(term[half:], scale)
    for k in range(far - 1, -1, -1):
        mark = waits(far - 1 - k, right)
        right, left = move(right, 1), move(left, -1)
        if mark is not None:
            right, left = after((right, left), mark)
        if k == far - 1:
            zero = jnp.zeros_like(right)
            right, left = jnp.concatenate([right, zero]), jnp.concatenate([zero, left])
        if k == 0:
            break
        right = narrow(wide(right, scale) + part(k), scale)
        left = narrow(wide(left, scale) + part(-k), scale)
    return wide(right, scale) + wide(left, scale) + part(0)


def step_of(index):
    return jnp.where(index == 3, 2, jnp.where(index == 2, 1, -index))


def final_kernel(lengths, *refs):
    own, (near, right, left), acts, (old, out, gs, acs, sems) = refs[:9], refs[9:12], refs[12:16], refs[16:]
    x, y, z, core = place()
    copies = []

    def fetch(source, row, count, whole, start):
        start = pl.multiple_of(start, PIECE // 2)
        copies.append(
            pltpu.make_async_copy(
                source.at[pl.ds(row, count), :], whole.at[pl.ds(start, count), :], sems.at[len(copies)]
            )
        )
        copies[-1].start()

    def fetch_grads(block, row, count, chunk, holder, into):
        grid_row, column = chunk // 4 + 2 * holder, lax.rem(chunk, 4)
        piece = lax.rem(y + step_of(grid_row) + Y, Y) * X + lax.rem(x + step_of(column) + X, X)
        fetch(block, row, count, gs, piece * PIECE + into)

    for i, step in enumerate((0, -1, 1, -2, 2, -3, 3)):
        chunk = lax.rem(z + step + Z, Z)
        fetch_grads(own[i], 0, PIECE, chunk, core, 0)
        fetch_grads(near, i * PIECE, PIECE, chunk, 1 - core, 0)
    far = lax.rem(z + Z // 2, Z)
    for holder, halves in ((core, own[7:]), (1 - core, (right, left))):
        for i, half in enumerate(halves):
            fetch_grads(half, 0, PIECE // 2, far, holder, i * (PIECE // 2))
    first_at, second_at = jnp.where(core == 0, x, y), jnp.where(core == 0, y, x)
    way = 1 - 2 * core
    for i, block in enumerate(acts):
        for k in range(4):
            piece = lax.rem(first_at + STEPS[i] + 4, 4) * 4 + lax.rem(second_at + STEPS[k] + 4, 4)
            theirs = piece - 9
            at = jnp.where(piece < 9, z - way * (piece // 2), z + way * (theirs // 2 + 1))
            odd = jnp.where(piece < 9, lax.rem(piece, 2), 1 - lax.rem(theirs + 16, 2))
            holder = jnp.where(odd == 0, core, 1 - core)
            fetch(block, k * PIECE, PIECE, acs, (lax.rem(at + Z, Z) * 2 + holder) * PIECE)
    for copy in copies:
        copy.wait()
    out[...] = jnp.zeros_like(out)
    row_count = gs.shape[0]
    tile = 128

    def add_example(first, offset, length, count):
        window = pl.ds(first, count)
        act = acs[window, :]
        places = first + lax.broadcasted_iota(jnp.int32, act.shape, 0)
        inside = (places >= offset) & (places < offset + length)
        act = jnp.where(inside, act.astype(jnp.float32), 0.0).astype(jnp.bfloat16)
        for start in range(0, out.shape[0], tile):
            projected = lax.dot_general(
                gs[window, start : start + tile],
                act,
                (((0,), (0,)), ((), ())),
                preferred_element_type=jnp.float32,
            )
            out[start : start + tile, :] += projected * projected

    def step(example, offset):
        length = lengths[example]
        first = jnp.minimum(offset // ALIGN * ALIGN, row_count - CAP)
        first = pl.multiple_of(first, ALIGN)
        fits = offset + length <= first + CAP

        @pl.when(fits)
        def _():
            add_example(first, offset, length, CAP)

        @pl.when(jnp.logical_not(fits))
        def _():
            add_example(first, offset, length, CAP + ALIGN)

        return offset + length

    lax.fori_loop(0, lengths.shape[0], step, jnp.int32(0))
    out[...] = 0.8 * old[...] + 0.2 * out[...] / lengths.shape[0]


def correct(lengths, grads, acts, old):
    rows = sum(b.shape[0] for b in acts)
    smem = pl.BlockSpec(memory_space=pltpu.SMEM)
    vmem = pl.BlockSpec(memory_space=pltpu.VMEM)
    hbm = pl.BlockSpec(memory_space=pltpu.HBM)
    return pl.pallas_call(
        final_kernel,
        out_shape=jax.ShapeDtypeStruct(old.shape, jnp.float32),
        in_specs=[smem] + [hbm] * (len(grads) + len(acts)) + [vmem],
        out_specs=vmem,
        scratch_shapes=[
            pltpu.VMEM((rows, grads[0].shape[1]), jnp.bfloat16),
            pltpu.VMEM((rows, acts[0].shape[1]), jnp.bfloat16),
            pltpu.SemaphoreType.DMA((2 * 9 + X * Y,)),
        ],
        compiler_params=pltpu.CompilerParams(vmem_limit_bytes=60 * 2**20),
    )(lengths, *grads, *acts, old)


def divide_kernel(y0, y12, right, left, basis, give, keep, y3, give_at, keep_at, sems):
    half = right.shape[0]
    y3[:half, :] = jnp.dot(right[...], basis[...], preferred_element_type=jnp.float32)
    y3[half:, :] = jnp.dot(left[...], basis[...], preferred_element_type=jnp.float32)
    rows = y0.shape[0] // 4
    core = place()[3]

    def piece(row, column, mine):
        i, k = (row, column) if mine == 0 else (column, row)
        block, start = ((y0, 0), (y12, 0), (y12, 4), (y3, 0))[i]
        return block[(start + k) * rows : (start + k + 1) * rows, :]

    for mine in range(2):

        @pl.when(core == mine)
        def _():
            for k in range(8):
                here = slice(k * rows, (k + 1) * rows)
                give_at[here, :] = piece(k // 4 + 2 - 2 * mine, k % 4, mine).astype(give.dtype)

    given = pltpu.make_async_copy(give_at, give, sems.at[0])
    given.start()
    for mine in range(2):

        @pl.when(core == mine)
        def _():
            for k in range(8):
                here = slice(k * rows, (k + 1) * rows)
                keep_at[here, :] = piece(k // 4 + 2 * mine, k % 4, mine)

    kept = pltpu.make_async_copy(keep_at, keep, sems.at[1])
    kept.start()
    given.wait()
    kept.wait()


def divide(done, right, left, basis):
    rows, columns = 2 * done[0].shape[0], basis.shape[1]
    vmem = pl.BlockSpec(memory_space=pltpu.VMEM)
    hbm = pl.BlockSpec(memory_space=pltpu.HBM)
    return pl.pallas_call(
        divide_kernel,
        out_shape=[
            jax.ShapeDtypeStruct((rows, columns), GIVE),
            jax.ShapeDtypeStruct((rows, columns), jnp.float32),
        ],
        in_specs=[vmem] * 5,
        out_specs=[hbm, hbm],
        scratch_shapes=[
            pltpu.VMEM(done[0].shape, jnp.float32),
            pltpu.VMEM((rows, columns), GIVE),
            pltpu.VMEM((rows, columns), jnp.float32),
            pltpu.SemaphoreType.DMA((2,)),
        ],
        compiler_params=pltpu.CompilerParams(vmem_limit_bytes=24 * 2**20),
        cost_estimate=pl.CostEstimate(
            flops=rows * basis.shape[0] * columns,
            bytes_accessed=16 * rows * columns,
            transcendentals=0,
        ),
    )(*done, right, left, basis)


def slab(array, index, count):
    rows = array.shape[0] // count
    return lax.dynamic_slice_in_dim(array, index % count * rows, rows)


def body(grads, acts, basis_out, basis_in, old_correction, lengths):
    x_at, y_at, z_at, core = place()
    first_at = jnp.where(core == 0, x_at, y_at)
    second_at = jnp.where(core == 0, y_at, x_at)

    half = grads.shape[0] // 2
    inner = gather4(move_first, grads[:half], grads[half:])
    outer = pack(inner[:4]), pack(inner[4:])
    blocks = gather4(move_second, *outer)
    done = [rotate(outer, basis_out), rotate(blocks[2:6], basis_out)]

    both = pack([acts, swap_cores(acts)])
    steps = [move_apart(both)]
    steps.append(move_apart(steps[-1]))
    steps += after([steps.pop()], done[0])
    steps.append(move_apart(steps[-1]))
    steps.append(move_apart(steps[-1][: acts.shape[0]]))
    passed = pack(steps)
    all_acts = [both, passed, swap_cores(passed)]
    act_part = rotate(all_acts, basis_in)
    act_terms = [narrow(slab(act_part, first_at + k, 4), ACT_SCALE) for k in (1, -1, 2)]
    give, keep = divide(done, *blocks[6:], basis_out)
    (got,) = after([swap_cores(give)], act_terms[0])
    act = {"moved": [move_first(t, k) for t, k in zip(act_terms, (1, -1, 2))]}

    def act_sums(step, sent):
        if step == 1:
            moved = after(act["moved"], sent)
            sums = sum((wide(t, ACT_SCALE) for t in moved), slab(act_part, first_at, 4))
            terms = [narrow(slab(sums, second_at + k, 4), ACT_SCALE) for k in (1, -1, 2)]
            act["moved"] = [move_second(t, k) for t, k in zip(terms, (1, -1, 2))]
            act["sums"] = sums
            return terms[0]
        if step == 2:
            moved = after(act["moved"], sent)
            sums = sum((wide(t, ACT_SCALE) for t in moved), slab(act["sums"], second_at, 4))
            sums = sums.astype(jnp.bfloat16)
            act["moved"] = [move_second(sums, k) for k in (1, -1, 2)]
            act["sums"] = sums
            return sums
        if step == 3:
            sums = pack([act["sums"], *after(act["moved"], sent)])
            act["blocks"] = [sums, *[move_first(sums, k) for k in (1, -1, 2)]]
            return sums
        return None

    mine = scatter_sum(
        move_z,
        lambda k: slab(keep, z_at + k, Z) + slab(got, z_at + k, Z).astype(jnp.float32),
        Z,
        GRAD_SCALE,
        act_sums,
    )
    act_blocks = act["blocks"]

    near, far = gather8(
        move_z,
        mine.astype(jnp.bfloat16),
        lambda step, blocks: act_blocks[1:] if step == 1 else None,
    )
    grad_blocks = [*near, *far, swap_cores(pack(near)), *map(swap_cores, far)]
    return correct(lengths, grad_blocks, act_blocks, old_correction)


def solution(mesh):
    in_specs = (
        P("out", "inp"),
        P("inp", "out"),
        P("inp", "out"),
        P("out", "inp"),
        P("out", "inp"),
        P(),
    )
    out_specs = P("out", "inp")
    return jax.shard_map(body, mesh=mesh, in_specs=in_specs, out_specs=out_specs, check_vma=False)
```

```python
import functools

import jax
import jax.numpy as jnp
from jax import lax
from jax.experimental import pallas as pl
from jax.experimental.pallas import tpu as pltpu
from jax.sharding import PartitionSpec as P

CAP = 256
X = Y = 4
Z = 8
PIECE = 128
ALIGN = 16
STEPS = (0, -1, 1, 2)
WIRE = jnp.float16
GIVE = jnp.bfloat16
GRAD_SCALE = 32.0
ACT_SCALE = 16.0


def place():
    out, inp = lax.axis_index("out"), lax.axis_index("inp")
    return lax.rem(out, X), out // X, inp // 2, lax.rem(inp, 2)


def move_plane(array, step, axes):
    mesh_out, mesh_inp = X * Y, 2 * Z
    pairs = []
    for y in range(Y):
        for x in range(X):
            near = {"x": y * X + (x + step) % X, "y": (y + step) % Y * X + x}
            for inp in range(mesh_inp):
                pairs.append(((y * X + x) * mesh_inp + inp, near[axes[inp % 2]] * mesh_inp + inp))
    return lax.ppermute(array, ("out", "inp"), pairs)


def move_first(array, step):
    return move_plane(array, step, "xy")


def move_second(array, step):
    return move_plane(array, step, "yx")


def move_z(array, step):
    pairs = [(z * 2 + c, (z + step) % Z * 2 + c) for z in range(Z) for c in range(2)]
    return lax.ppermute(array, "inp", pairs)


def move_apart(array):
    pairs = [(z * 2 + c, (z + 1 - 2 * c) % Z * 2 + c) for z in range(Z) for c in range(2)]
    return lax.ppermute(array, "inp", pairs)


def swap_cores(array):
    pairs = [(z * 2 + c, z * 2 + 1 - c) for z in range(Z) for c in range(2)]
    return lax.ppermute(array, "inp", pairs)


def gather4(move, first, second):
    right, left = move(first, 1), move(second, -1)
    right_rest, left_rest = move(second, 1), move(first, -1)
    right2, left2 = move(right, 1), move(left, -1)
    return [first, second, right, right_rest, left_rest, left, right2, left2]


def gather8(move, block, waits):
    half = block.shape[0] // 2
    right, left = block, block
    blocks = [block]
    for step in range(3):
        right, left = move(right, 1), move(left, -1)
        blocks += [right, left]
        mark = waits(step, blocks)
        if mark is not None:
            right, left = after((right, left), mark)
    return blocks, [move(right[:half], 1), move(left[half:], -1)]


def pack_kernel(*refs):
    *parts, out, sems = refs
    copies, row = [], 0
    for i, part in enumerate(parts):
        rows = pl.ds(row, part.shape[0])
        copies.append(pltpu.make_async_copy(part, out.at[rows, :], sems.at[i]))
        row += part.shape[0]
    for copy in copies:
        copy.start()
    for copy in copies:
        copy.wait()


def pack(blocks):
    rows = sum(b.shape[0] for b in blocks)
    like = blocks[0]
    anywhere = pl.BlockSpec(memory_space=pl.ANY)
    hbm = pl.BlockSpec(memory_space=pltpu.HBM)
    return pl.pallas_call(
        pack_kernel,
        out_shape=jax.ShapeDtypeStruct((rows, like.shape[1]), like.dtype),
        in_specs=[anywhere] * len(blocks),
        out_specs=hbm,
        scratch_shapes=[pltpu.SemaphoreType.DMA((len(blocks),))],
        compiler_params=pltpu.CompilerParams(vmem_limit_bytes=2**20),
        cost_estimate=pl.CostEstimate(
            flops=0, bytes_accessed=4 * rows * like.shape[1], transcendentals=0
        ),
    )(*blocks)


def rotate_kernel(*refs):
    *blocks, basis, out, total, sems = refs
    copies, row = [], 0
    for i, block in enumerate(blocks):
        rows = pl.ds(row, block.shape[0])
        total[rows, :] = jnp.dot(block[...], basis[...], preferred_element_type=jnp.float32)
        copies.append(pltpu.make_async_copy(total.at[rows, :], out.at[rows, :], sems.at[i]))
        copies[-1].start()
        row += block.shape[0]
    for copy in copies:
        copy.wait()


def rotate(blocks, basis):
    rows, columns = sum(b.shape[0] for b in blocks), basis.shape[1]
    vmem = pl.BlockSpec(memory_space=pltpu.VMEM)
    size = 2 * (rows + columns) * basis.shape[0] + 4 * rows * columns
    return pl.pallas_call(
        rotate_kernel,
        out_shape=jax.ShapeDtypeStruct((rows, columns), jnp.float32),
        in_specs=[vmem] * (len(blocks) + 1),
        out_specs=pl.BlockSpec(memory_space=pltpu.HBM),
        scratch_shapes=[
            pltpu.VMEM((rows, columns), jnp.float32),
            pltpu.SemaphoreType.DMA((len(blocks),)),
        ],
        compiler_params=pltpu.CompilerParams(vmem_limit_bytes=size + 4 * 2**20),
        cost_estimate=pl.CostEstimate(
            flops=2 * rows * basis.shape[0] * columns, bytes_accessed=size, transcendentals=0
        ),
    )(*blocks, basis)


def narrow(array, scale):
    return (array * scale).astype(WIRE)


def wide(array, scale):
    return array.astype(jnp.float32) * (1.0 / scale)


def after(pair, mark):
    marks = mark if isinstance(mark, list) else [mark]
    return lax.optimization_barrier((*pair, *marks))[: len(pair)]


def scatter_sum(move, part, count, scale, waits):
    far = count // 2
    term = part(far)
    half = term.shape[0] // 2
    right, left = narrow(term[:half], scale), narrow(term[half:], scale)
    for k in range(far - 1, -1, -1):
        mark = waits(far - 1 - k, right)
        right, left = move(right, 1), move(left, -1)
        if mark is not None:
            right, left = after((right, left), mark)
        if k == far - 1:
            zero = jnp.zeros_like(right)
            right, left = jnp.concatenate([right, zero]), jnp.concatenate([zero, left])
        if k == 0:
            break
        right = narrow(wide(right, scale) + part(k), scale)
        left = narrow(wide(left, scale) + part(-k), scale)
    return wide(right, scale) + wide(left, scale) + part(0)


def step_of(index):
    return jnp.where(index == 3, 2, jnp.where(index == 2, 1, -index))


def final_kernel(lengths, *refs):
    own, (near, *rest), acts, (old, out, gs, acs, sems) = refs[:9], refs[9:14], refs[14:18], refs[18:]
    x, y, z, core = place()
    copies = []

    def fetch(source, row, count, whole, start):
        start = pl.multiple_of(start, PIECE // 2)
        copies.append(
            pltpu.make_async_copy(
                source.at[pl.ds(row, count), :], whole.at[pl.ds(start, count), :], sems.at[len(copies)]
            )
        )
        copies[-1].start()

    def fetch_grads(block, row, count, chunk, holder, into):
        grid_row, column = chunk // 4 + 2 * holder, lax.rem(chunk, 4)
        piece = lax.rem(y + step_of(grid_row) + Y, Y) * X + lax.rem(x + step_of(column) + X, X)
        fetch(block, row, count, gs, piece * PIECE + into)

    for i, step in enumerate((0, -1, 1, -2, 2, -3, 3)):
        chunk = lax.rem(z + step + Z, Z)
        fetch_grads(own[i], 0, PIECE, chunk, core, 0)
        theirs, row = (near, i * PIECE) if i < 5 else (rest[i - 5], 0)
        fetch_grads(theirs, row, PIECE, chunk, 1 - core, 0)
    far = lax.rem(z + Z // 2, Z)
    for holder, halves in ((core, own[7:]), (1 - core, rest[2:])):
        for i, half in enumerate(halves):
            fetch_grads(half, 0, PIECE // 2, far, holder, i * (PIECE // 2))
    first_at, second_at = jnp.where(core == 0, x, y), jnp.where(core == 0, y, x)
    way = 1 - 2 * core
    for i, block in enumerate(acts):
        for k in range(4):
            piece = lax.rem(first_at + STEPS[i] + 4, 4) * 4 + lax.rem(second_at + STEPS[k] + 4, 4)
            theirs = piece - 9
            at = jnp.where(piece < 9, z - way * (piece // 2), z + way * (theirs // 2 + 1))
            odd = jnp.where(piece < 9, lax.rem(piece, 2), 1 - lax.rem(theirs + 16, 2))
            holder = jnp.where(odd == 0, core, 1 - core)
            fetch(block, k * PIECE, PIECE, acs, (lax.rem(at + Z, Z) * 2 + holder) * PIECE)
    for copy in copies:
        copy.wait()
    out[...] = jnp.zeros_like(out)
    row_count = gs.shape[0]
    tile = 128

    def add_example(first, offset, length, count):
        window = pl.ds(first, count)
        act = acs[window, :]
        places = first + lax.broadcasted_iota(jnp.int32, act.shape, 0)
        inside = (places >= offset) & (places < offset + length)
        act = jnp.where(inside, act.astype(jnp.float32), 0.0).astype(jnp.bfloat16)
        for start in range(0, out.shape[0], tile):
            projected = lax.dot_general(
                gs[window, start : start + tile],
                act,
                (((0,), (0,)), ((), ())),
                preferred_element_type=jnp.float32,
            )
            out[start : start + tile, :] += projected * projected

    def step(example, offset):
        length = lengths[example]
        first = jnp.minimum(offset // ALIGN * ALIGN, row_count - CAP)
        first = pl.multiple_of(first, ALIGN)
        fits = offset + length <= first + CAP

        @pl.when(fits)
        def _():
            add_example(first, offset, length, CAP)

        @pl.when(jnp.logical_not(fits))
        def _():
            add_example(first, offset, length, CAP + ALIGN)

        return offset + length

    lax.fori_loop(0, lengths.shape[0], step, jnp.int32(0))
    out[...] = 0.8 * old[...] + 0.2 * out[...] / lengths.shape[0]


def correct(lengths, grads, acts, old):
    rows = sum(b.shape[0] for b in acts)
    smem = pl.BlockSpec(memory_space=pltpu.SMEM)
    vmem = pl.BlockSpec(memory_space=pltpu.VMEM)
    hbm = pl.BlockSpec(memory_space=pltpu.HBM)
    return pl.pallas_call(
        final_kernel,
        out_shape=jax.ShapeDtypeStruct(old.shape, jnp.float32),
        in_specs=[smem] + [hbm] * (len(grads) + len(acts)) + [vmem],
        out_specs=vmem,
        scratch_shapes=[
            pltpu.VMEM((rows, grads[0].shape[1]), jnp.bfloat16),
            pltpu.VMEM((rows, acts[0].shape[1]), jnp.bfloat16),
            pltpu.SemaphoreType.DMA((2 * 9 + X * Y,)),
        ],
        compiler_params=pltpu.CompilerParams(vmem_limit_bytes=60 * 2**20),
    )(lengths, *grads, *acts, old)


def divide_kernel(y0, y12, right, left, basis, give, keep, y3, give_at, keep_at, sems):
    half = right.shape[0]
    y3[:half, :] = jnp.dot(right[...], basis[...], preferred_element_type=jnp.float32)
    y3[half:, :] = jnp.dot(left[...], basis[...], preferred_element_type=jnp.float32)
    rows = y0.shape[0] // 4
    core = place()[3]

    def piece(row, column, mine):
        i, k = (row, column) if mine == 0 else (column, row)
        block, start = ((y0, 0), (y12, 0), (y12, 4), (y3, 0))[i]
        return block[(start + k) * rows : (start + k + 1) * rows, :]

    for mine in range(2):

        @pl.when(core == mine)
        def _():
            for k in range(8):
                here = slice(k * rows, (k + 1) * rows)
                give_at[here, :] = piece(k // 4 + 2 - 2 * mine, k % 4, mine).astype(give.dtype)

    given = pltpu.make_async_copy(give_at, give, sems.at[0])
    given.start()
    for mine in range(2):

        @pl.when(core == mine)
        def _():
            for k in range(8):
                here = slice(k * rows, (k + 1) * rows)
                keep_at[here, :] = piece(k // 4 + 2 * mine, k % 4, mine)

    kept = pltpu.make_async_copy(keep_at, keep, sems.at[1])
    kept.start()
    given.wait()
    kept.wait()


def divide(done, right, left, basis):
    rows, columns = 2 * done[0].shape[0], basis.shape[1]
    vmem = pl.BlockSpec(memory_space=pltpu.VMEM)
    hbm = pl.BlockSpec(memory_space=pltpu.HBM)
    return pl.pallas_call(
        divide_kernel,
        out_shape=[
            jax.ShapeDtypeStruct((rows, columns), GIVE),
            jax.ShapeDtypeStruct((rows, columns), jnp.float32),
        ],
        in_specs=[vmem] * 5,
        out_specs=[hbm, hbm],
        scratch_shapes=[
            pltpu.VMEM(done[0].shape, jnp.float32),
            pltpu.VMEM((rows, columns), GIVE),
            pltpu.VMEM((rows, columns), jnp.float32),
            pltpu.SemaphoreType.DMA((2,)),
        ],
        compiler_params=pltpu.CompilerParams(vmem_limit_bytes=24 * 2**20),
        cost_estimate=pl.CostEstimate(
            flops=rows * basis.shape[0] * columns,
            bytes_accessed=16 * rows * columns,
            transcendentals=0,
        ),
    )(*done, right, left, basis)


def slab(array, index, count):
    rows = array.shape[0] // count
    return lax.dynamic_slice_in_dim(array, index % count * rows, rows)


def body(grads, acts, basis_out, basis_in, old_correction, lengths):
    x_at, y_at, z_at, core = place()
    first_at = jnp.where(core == 0, x_at, y_at)
    second_at = jnp.where(core == 0, y_at, x_at)

    half = grads.shape[0] // 2
    inner = gather4(move_first, grads[:half], grads[half:])
    outer = pack(inner[:4]), pack(inner[4:])
    blocks = gather4(move_second, *outer)
    done = [rotate(outer, basis_out), rotate(blocks[2:6], basis_out)]

    both = pack([acts, swap_cores(acts)])
    steps = [move_apart(both)]
    steps.append(move_apart(steps[-1]))
    steps += after([steps.pop()], done[0])
    steps.append(move_apart(steps[-1]))
    steps.append(move_apart(steps[-1][: acts.shape[0]]))
    passed = pack(steps)
    all_acts = [both, passed, swap_cores(passed)]
    act_part = rotate(all_acts, basis_in)
    act_terms = [narrow(slab(act_part, first_at + k, 4), ACT_SCALE) for k in (1, -1, 2)]
    last = after(blocks[6:], act_terms[0])
    give, keep = divide(done, *last, basis_out)
    got = swap_cores(give)
    act = {"moved": [move_first(t, k) for t, k in zip(act_terms, (1, -1, 2))]}

    def act_sums(step, sent):
        if step == 1:
            moved = after(act["moved"], sent)
            sums = sum((wide(t, ACT_SCALE) for t in moved), slab(act_part, first_at, 4))
            terms = [narrow(slab(sums, second_at + k, 4), ACT_SCALE) for k in (1, -1, 2)]
            act["moved"] = [move_second(t, k) for t, k in zip(terms, (1, -1, 2))]
            act["sums"] = sums
            return terms[0]
        if step == 2:
            moved = after(act["moved"], sent)
            sums = sum((wide(t, ACT_SCALE) for t in moved), slab(act["sums"], second_at, 4))
            sums = sums.astype(jnp.bfloat16)
            act["moved"] = [move_second(sums, k) for k in (1, -1, 2)]
            act["sums"] = sums
            return sums
        if step == 3:
            sums = pack([act["sums"], *after(act["moved"], sent)])
            act["blocks"] = [sums, *[move_first(sums, k) for k in (1, -1, 2)]]
            return sums
        return None

    mine = scatter_sum(
        move_z,
        lambda k: slab(keep, z_at + k, Z) + slab(got, z_at + k, Z).astype(jnp.float32),
        Z,
        GRAD_SCALE,
        act_sums,
    )
    act_blocks = act["blocks"]

    near, far = gather8(
        move_z,
        mine.astype(jnp.bfloat16),
        lambda step, blocks: act_blocks[1:] if step == 1 else None,
    )
    early = pack(after(near[:5], act_blocks[1:]))
    grad_blocks = [*near, *far, swap_cores(early), *map(swap_cores, near[5:] + far)]
    return correct(lengths, grad_blocks, act_blocks, old_correction)


def solution(mesh):
    in_specs = (
        P("out", "inp"),
        P("inp", "out"),
        P("inp", "out"),
        P("out", "inp"),
        P("out", "inp"),
        P(),
    )
    out_specs = P("out", "inp")
    return jax.shard_map(body, mesh=mesh, in_specs=in_specs, out_specs=out_specs, check_vma=False)
```
